32 devices in a mesh: tensor: 4 (over y, core), fsdp: 4 (over z), dp: 2 (over x).
Axes of the slice: x: 2, y: 2, z: 4, core: 2. Of those that a mesh axis runs over, the one named last changes fastest.
Arguments:
- tokens: bfloat16 [256, 8192], P(('tensor', 'dp'), 'fsdp'), may hold values from -6 to 6
- gate_weight: bfloat16 [8192, 28672], P('fsdp', 'tensor'), may hold values from -0.0625 to 0.0625
- up_weight: bfloat16 [8192, 28672], P('fsdp', 'tensor'), may hold values from -0.0625 to 0.0625
- down_weight: bfloat16 [28672, 8192], P('tensor', 'fsdp'), may hold values from -0.03125 to 0.03125
- keep_bits: int32 [256, 512], P(('tensor', 'dp'), 'fsdp'), may hold values from 0 to 65535
Outputs:
- mixed: bfloat16 [256, 8192], P(('tensor', 'dp'), 'fsdp')
The draws below stay inside these ranges and needn't reach their ends.
Inputs may be any that keep to these rules, and one draw needn't show every extreme that they name: `keep_bits`: bit j of word c of a row is the keep flag of column 16 c + j of that row; every 16-bit pattern can occur.
All inputs are finite; a program needn't handle non-finite values.
Results may differ from the reference program's by a relative error of at most 0.0049.
Values may be sent and summed in bfloat16 or wider, within the bound.
No kernel may reach another device: no remote copies, remote signals or barrier semaphores. Data moves between devices by JAX's collectives and lax.ppermute only.
A program may use at most 192 MiB of HBM per device.

```python
import jax
import jax.numpy as jnp

D = 8192
FF = 28672
TOKENS = 256


def set_ends(values, rng, least, top_value):
    dims = values.shape
    place = [jax.random.randint(jax.random.fold_in(rng, axis), (), 0, dims[axis]) for axis in range(len(dims))]
    values = values.at[tuple(place)].set(least)
    longest = dims.index(max(dims))
    place[longest] = (place[longest] + 1) % dims[longest]
    return values.at[tuple(place)].set(top_value)


def shard_levels(key, extent, pieces, low, high):
    def one(position, shards_of):
        heights = jax.random.uniform(jax.random.fold_in(jax.random.fold_in(key, 6), position), (shards_of,), jnp.float32, low / len(pieces), high / len(pieces))
        return jnp.repeat(jnp.exp(heights), extent[position] // shards_of).reshape((-1,) + (1,) * (len(extent) - position - 1))

    gain = one(*pieces[0])
    for cut in pieces[1:]:
        gain = gain * one(*cut)
    return gain


def centred(stream_key, dims, width, most, shards=(), kind=jnp.bfloat16):
    result = width * jax.random.normal(stream_key, dims, jnp.float32)
    if shards:
        result = result * shard_levels(stream_key, dims, shards, -0.22, 0.18)
    return jnp.clip(result, -most, most).astype(kind)


def setup_inputs(seed: int = 0) -> dict:
    key_of = jax.random.split(jax.random.key(seed), 6)
    return {
        "tokens": centred(key_of[0], (TOKENS, D), 1.0, 6.0, ((0, 8), (1, 4))),
        "gate_weight": centred(key_of[1], (D, FF), D ** -0.5, 0.0625, ((0, 4), (1, 4))),
        "up_weight": centred(key_of[2], (D, FF), D ** -0.5, 0.0625, ((0, 4), (1, 4))),
        "down_weight": centred(key_of[3], (FF, D), FF ** -0.5, 0.03125, ((0, 4), (1, 4))),
        "keep_bits": set_ends(jax.random.randint(key_of[4], (TOKENS, D // 16), 0, 65536), jax.random.fold_in(key_of[4], 1), 0, 65535).astype(jnp.int32),
    }


def reference(tokens, gate_weight, up_weight, down_weight, keep_bits):
    gate = jnp.dot(tokens, gate_weight, preferred_element_type=jnp.float32)
    up = jnp.dot(tokens, up_weight, preferred_element_type=jnp.float32)
    hidden = (jax.nn.silu(gate) * up).astype(jnp.bfloat16)
    projected = jnp.dot(hidden, down_weight, preferred_element_type=jnp.float32)
    shifts = jnp.arange(16, dtype=jnp.int32)
    keep = jnp.right_shift(keep_bits[:, :, None], shifts[None, None, :]) & 1
    keep = keep.reshape(tokens.shape[0], D).astype(jnp.float32)
    return (2.0 * keep * projected).astype(jnp.bfloat16)
```

```python
import jax
import jax.numpy as jnp
from jax import lax
from jax.experimental import pallas as pl
from jax.experimental.pallas import tpu as pltpu
from jax.sharding import PartitionSpec as P

F32, BF16 = jnp.float32, jnp.bfloat16
SHARES = (1, 3, 3, 3, 3, 1)
VMEM_LIMIT = 48 << 20


def swap(size, bit):
    return [(i, i ^ bit) for i in range(size)]


def unit_tile(units, shares):
    tile = units // sum(shares)
    return tile if tile * sum(shares) == units and tile % 128 == 0 else 0


def up_kernel(x, g, u, *rest):
    narrow, wide = rest[-2:]
    a = jnp.dot(x[...], g[...], preferred_element_type=F32)
    b = jnp.dot(x[...], u[...], preferred_element_type=F32)
    narrow[0], narrow[1] = a.astype(BF16), b.astype(BF16)
    wide[0], wide[1] = a, b


def partial_sums(x, gate, up, first, count, tile, after):
    rows, depth = x.shape
    units = count * tile
    weight = pl.BlockSpec((depth, tile), lambda i: (0, first + i))
    out = pl.BlockSpec((2, rows, tile), lambda i: (0, 0, i))
    return pl.pallas_call(
        up_kernel,
        grid=(count,),
        in_specs=[pl.BlockSpec((rows, depth), lambda i: (0, 0)), weight, weight] + [pl.BlockSpec(memory_space=pl.ANY)] * len(after),
        out_specs=[out, out],
        out_shape=[
            jax.ShapeDtypeStruct((2, rows, units), BF16),
            jax.ShapeDtypeStruct((2, rows, units), F32),
        ],
        compiler_params=pltpu.CompilerParams(vmem_limit_bytes=VMEM_LIMIT),
        cost_estimate=pl.CostEstimate(
            flops=4 * rows * depth * units, bytes_accessed=4 * depth * units, transcendentals=0
        ),
        name="gate_up",
    )(x, gate, up, *after)


def down_kernel(inner, own, other, w, base, total):
    h = jnp.where(inner[0] > 0, own[...], other[...])
    part = jnp.dot(h, w[...], preferred_element_type=F32)

    @pl.when(pl.program_id(0) == 0)
    def _():
        total[...] = base[...] + part

    @pl.when(pl.program_id(0) > 0)
    def _():
        total[...] += part


def add_down(inner, own, other, down, base, first, count, tile):
    rows, width = base.shape
    piece = pl.BlockSpec((rows, tile), lambda i, s: (0, i))
    whole = pl.BlockSpec((rows, width), lambda i, s: (0, 0))
    return pl.pallas_call(
        down_kernel,
        grid_spec=pltpu.PrefetchScalarGridSpec(
            num_scalar_prefetch=1,
            grid=(count,),
            in_specs=[piece, piece, pl.BlockSpec((tile, width), lambda i, s: (first + i, 0)), whole],
            out_specs=whole,
        ),
        out_shape=jax.ShapeDtypeStruct((rows, width), F32),
        compiler_params=pltpu.CompilerParams(vmem_limit_bytes=VMEM_LIMIT),
        cost_estimate=pl.CostEstimate(
            flops=2 * rows * width * count * tile,
            bytes_accessed=2 * width * count * tile,
            transcendentals=0,
        ),
        name="down",
    )(inner, own, other, down, base)


def keep_scale(keep_bits, width):
    shifts = jnp.arange(16, dtype=jnp.int32)
    keep = jnp.right_shift(keep_bits[:, :, None], shifts[None, None, :]) & 1
    return 2.0 * keep.reshape(keep_bits.shape[0], width).astype(F32)


def line_of_four(tensor):
    def shards(tokens, gate, up, down, keep_bits):
        rows = tokens.shape[0]
        units, width = down.shape
        tile = unit_tile(units, SHARES)
        inner = ((lax.axis_index("fsdp") + 1) // 2 == 1).astype(jnp.int32).reshape(1)
        scale = keep_scale(keep_bits, width)
        x = tokens
        bits = [1 << b for b in reversed(range((tensor - 1).bit_length()))]
        for bit in bits:
            x = jnp.concatenate([x, lax.ppermute(x, "tensor", swap(tensor, bit))], axis=0)
        total = jnp.zeros((x.shape[0], width), F32)
        count = len(SHARES)
        firsts = [sum(SHARES[:c]) for c in range(count)]
        wide, heard, side, crossed, hidden, given = ([None] * count for _ in range(6))

        def send_out(c):
            after = [side[c - 2][1]] if c >= 2 else []
            narrow, wide[c] = partial_sums(x, gate, up, firsts[c], SHARES[c], tile, after)
            heard[c] = lax.ppermute(narrow, "fsdp", [(0, 1), (3, 2)])

        def cross(c):
            added = wide[c] + heard[c].astype(F32)
            side[c] = (added, added.astype(BF16))
            crossed[c] = lax.ppermute(side[c][1], "fsdp", [(1, 2), (2, 1)])

        def give(c):
            both = side[c][0] + crossed[c].astype(F32)
            hidden[c] = (jax.nn.silu(both[0]) * both[1]).astype(BF16)
            given[c] = lax.ppermute(hidden[c], "fsdp", [(1, 0), (2, 3)])

        for c in range(count + 3):
            if c < count:
                send_out(c)
            if 0 <= c - 1 < count:
                cross(c - 1)
            if 0 <= c - 2 < count:
                give(c - 2)
            if 0 <= c - 3 < count:
                p = c - 3
                total = add_down(inner, hidden[p], given[p], down, total, firsts[p], SHARES[p], tile)
        for step, bit in enumerate(reversed(bits)):
            half = total.shape[0] // 2
            away = total[half:]
            away = away if step == 0 else away.astype(BF16)
            total = total[:half] + lax.ppermute(away, "tensor", swap(tensor, bit)).astype(F32)
        return (scale * total).astype(BF16)

    return shards


def any_line(tokens, gate, up, down, keep_bits):
    units, width = down.shape
    x = lax.all_gather(tokens, "tensor", axis=0, tiled=True)
    both = jnp.concatenate(
        [jnp.dot(x, gate, preferred_element_type=F32), jnp.dot(x, up, preferred_element_type=F32)], axis=1
    )
    both = lax.psum_scatter(both, "fsdp", scatter_dimension=0, tiled=True)
    hidden = (jax.nn.silu(both[:, :units]) * both[:, units:]).astype(BF16)
    hidden = lax.all_gather(hidden, "fsdp", axis=0, tiled=True)
    total = jnp.dot(hidden, down, preferred_element_type=F32)
    total = lax.psum_scatter(total, "tensor", scatter_dimension=0, tiled=True)
    return (keep_scale(keep_bits, width) * total).astype(BF16)


def solution(mesh):
    tensor, fsdp = mesh.shape["tensor"], mesh.shape["fsdp"]

    def shards(tokens, gate, up, down, keep_bits):
        cut = fsdp == 4 and tensor & (tensor - 1) == 0 and unit_tile(down.shape[0], SHARES)
        return (line_of_four(tensor) if cut else any_line)(tokens, gate, up, down, keep_bits)

    return jax.shard_map(
        shards,
        mesh=mesh,
        in_specs=(
            P(("tensor", "dp"), "fsdp"),
            P("fsdp", "tensor"),
            P("fsdp", "tensor"),
            P("tensor", "fsdp"),
            P(("tensor", "dp"), "fsdp"),
        ),
        out_specs=P(("tensor", "dp"), "fsdp"),
        check_vma=False,
    )
```

```python
import jax
import jax.numpy as jnp
from jax import lax
from jax.experimental import pallas as pl
from jax.experimental.pallas import tpu as pltpu
from jax.sharding import PartitionSpec as P

F32, BF16 = jnp.float32, jnp.bfloat16
SHARES = (1, 5, 6, 6, 5, 4, 1)
SLOTS = 4
VMEM_LIMIT = 40 << 20


def swap(size, bit):
    return [(i, i ^ bit) for i in range(size)]


def unit_tile(units, shares):
    tile = units // sum(shares)
    return tile if tile * sum(shares) == units and tile % 128 == 0 else 0


def stream(count, copies, work):
    for i in range(min(SLOTS, count)):
        for copy in copies(i, i):
            copy.start()

    def step(i, _):
        slot = lax.rem(i, SLOTS)
        for copy in copies(i, slot):
            copy.wait()
        work(i, slot)

        @pl.when(i + SLOTS < count)
        def _():
            for copy in copies(i + SLOTS, slot):
                copy.start()

        return 0

    lax.fori_loop(0, count, step, 0)


def up_kernel(first, count, tile, pieces, *refs):
    parts, (gate, up) = refs[:pieces], refs[pieces : pieces + 2]
    outs, (x, held, sems) = refs[:-3], refs[-3:]
    narrow, wide = outs[-2:] if pieces == 1 else outs[-3:-1]

    def copies(i, slot):
        columns = pl.ds(pl.multiple_of((first + i) * tile, tile), tile)
        return [
            pltpu.make_async_copy(w.at[:, columns], held.at[slot, j], sems.at[slot, j])
            for j, w in enumerate((gate, up))
        ]

    row = 0
    for part in parts:
        x[row : row + part.shape[0]] = part[...]
        row += part.shape[0]
    if pieces > 1:
        outs[-1][...] = x[...]

    def work(i, slot):
        columns = pl.ds(pl.multiple_of(i * tile, tile), tile)
        for j in range(2):
            part = jnp.dot(x[...], held[slot, j], preferred_element_type=F32)
            narrow[j, :, columns] = part.astype(BF16)
            wide[j, :, columns] = part

    stream(count, copies, work)


def partial_sums(parts, gate, up, first, count, tile, after):
    depth = gate.shape[0]
    rows = sum(part.shape[0] for part in parts)
    units = count * tile
    in_vmem, anywhere = pl.BlockSpec(memory_space=pltpu.VMEM), pl.BlockSpec(memory_space=pl.ANY)
    out_shape = [jax.ShapeDtypeStruct((2, rows, units), BF16), jax.ShapeDtypeStruct((2, rows, units), F32)]
    if len(parts) > 1:
        out_shape.append(jax.ShapeDtypeStruct((rows, depth), BF16))
    return pl.pallas_call(
        lambda *refs: up_kernel(first, count, tile, len(parts), *refs),
        in_specs=[in_vmem] * len(parts) + [anywhere] * (2 + len(after)),
        out_specs=[in_vmem] * len(out_shape),
        out_shape=out_shape,
        scratch_shapes=[
            pltpu.VMEM((rows, depth), BF16),
            pltpu.VMEM((SLOTS, 2, depth, tile), BF16),
            pltpu.SemaphoreType.DMA((SLOTS, 2)),
        ],
        compiler_params=pltpu.CompilerParams(vmem_limit_bytes=VMEM_LIMIT),
        name="gate_up",
    )(*parts, gate, up, *after)


def down_kernel(first, count, tile, inner, own, other, w, base, total, held, sems):
    def copies(i, slot):
        rows = pl.ds(pl.multiple_of((first + i) * tile, tile), tile)
        return [pltpu.make_async_copy(w.at[rows], held.at[slot], sems.at[slot])]

    def work(i, slot):
        columns = pl.ds(pl.multiple_of(i * tile, tile), tile)
        h = jnp.where(inner[0] > 0, own[:, columns], other[:, columns])
        total[...] += jnp.dot(h, held[slot], preferred_element_type=F32)

    total[...] = base[...]
    stream(count, copies, work)


def add_down(inner, own, other, down, base, first, count, tile):
    rows, width = base.shape
    in_vmem = pl.BlockSpec(memory_space=pltpu.VMEM)
    return pl.pallas_call(
        lambda *refs: down_kernel(first, count, tile, *refs),
        in_specs=[
            pl.BlockSpec(memory_space=pltpu.SMEM),
            in_vmem,
            in_vmem,
            pl.BlockSpec(memory_space=pl.ANY),
            in_vmem,
        ],
        out_specs=in_vmem,
        out_shape=jax.ShapeDtypeStruct((rows, width), F32),
        scratch_shapes=[pltpu.VMEM((SLOTS, tile, width), BF16), pltpu.SemaphoreType.DMA((SLOTS,))],
        compiler_params=pltpu.CompilerParams(vmem_limit_bytes=VMEM_LIMIT),
        name="down",
    )(inner, own, other, down, base)


def keep_scale(keep_bits, width):
    shifts = jnp.arange(16, dtype=jnp.int32)
    keep = jnp.right_shift(keep_bits[:, :, None], shifts[None, None, :]) & 1
    return 2.0 * keep.reshape(keep_bits.shape[0], width).astype(F32)


def line_of_four(tensor):
    def shards(tokens, gate, up, down, keep_bits):
        rows = tokens.shape[0]
        units, width = down.shape
        tile = unit_tile(units, SHARES)
        inner = ((lax.axis_index("fsdp") + 1) // 2 == 1).astype(jnp.int32).reshape(1)
        scale = keep_scale(keep_bits, width)
        parts = [tokens]
        bits = [1 << b for b in reversed(range((tensor - 1).bit_length()))]
        for bit in bits:
            parts = parts + [lax.ppermute(part, "tensor", swap(tensor, bit)) for part in parts]
        total = [jnp.zeros((rows * tensor, width), F32)]
        count = len(SHARES)
        firsts = [sum(SHARES[:c]) for c in range(count)]
        wide, heard, side, crossed, hidden, given = ([None] * count for _ in range(6))

        def send_out(c):
            after = [side[c - 2][1]] if c >= 2 else []
            after += [crossed[c - 3]] if c >= 3 else []
            after += [total[0]] if c >= 4 else []
            out = partial_sums(parts, gate, up, firsts[c], SHARES[c], tile, after)
            narrow, wide[c] = out[:2]
            parts[:] = out[2:] or parts
            heard[c] = lax.ppermute(narrow, "fsdp", [(0, 1), (3, 2)])

        def cross(c):
            added = wide[c] + heard[c].astype(F32)
            side[c] = (added, added.astype(BF16))
            crossed[c] = lax.ppermute(side[c][1], "fsdp", [(1, 2), (2, 1)])

        def give(c):
            both = side[c][0] + crossed[c].astype(F32)
            hidden[c] = (jax.nn.silu(both[0]) * both[1]).astype(BF16)
            given[c] = lax.ppermute(hidden[c], "fsdp", [(1, 0), (2, 3)])

        for c in range(count + 3):
            if c < count:
                send_out(c)
            if 0 <= c - 1 < count:
                cross(c - 1)
            if 0 <= c - 2 < count:
                give(c - 2)
            if 0 <= c - 3 < count:
                p = c - 3
                total[0] = add_down(inner, hidden[p], given[p], down, total[0], firsts[p], SHARES[p], tile)
        total = total[0]
        for step, bit in enumerate(reversed(bits)):
            half = total.shape[0] // 2
            away = total[half:]
            away = away if step == 0 else away.astype(BF16)
            total = total[:half] + lax.ppermute(away, "tensor", swap(tensor, bit)).astype(F32)
        return (scale * total).astype(BF16)

    return shards


def any_line(tokens, gate, up, down, keep_bits):
    units, width = down.shape
    x = lax.all_gather(tokens, "tensor", axis=0, tiled=True)
    both = jnp.concatenate(
        [jnp.dot(x, gate, preferred_element_type=F32), jnp.dot(x, up, preferred_element_type=F32)], axis=1
    )
    both = lax.psum_scatter(both, "fsdp", scatter_dimension=0, tiled=True)
    hidden = (jax.nn.silu(both[:, :units]) * both[:, units:]).astype(BF16)
    hidden = lax.all_gather(hidden, "fsdp", axis=0, tiled=True)
    total = jnp.dot(hidden, down, preferred_element_type=F32)
    total = lax.psum_scatter(total, "tensor", scatter_dimension=0, tiled=True)
    return (keep_scale(keep_bits, width) * total).astype(BF16)


def solution(mesh):
    tensor, fsdp = mesh.shape["tensor"], mesh.shape["fsdp"]

    def shards(tokens, gate, up, down, keep_bits):
        cut = fsdp == 4 and tensor & (tensor - 1) == 0 and unit_tile(down.shape[0], SHARES)
        return (line_of_four(tensor) if cut else any_line)(tokens, gate, up, down, keep_bits)

    return jax.shard_map(
        shards,
        mesh=mesh,
        in_specs=(
            P(("tensor", "dp"), "fsdp"),
            P("fsdp", "tensor"),
            P("fsdp", "tensor"),
            P("tensor", "fsdp"),
            P(("tensor", "dp"), "fsdp"),
        ),
        out_specs=P(("tensor", "dp"), "fsdp"),
        check_vma=False,
    )
```

```python
import jax
import jax.numpy as jnp
from jax import lax
from jax.experimental import pallas as pl
from jax.experimental.pallas import tpu as pltpu
from jax.sharding import PartitionSpec as P

F32, BF16 = jnp.float32, jnp.bfloat16
SHARES = (1, 5, 6, 6, 4, 4, 2)
LAG = 3
SLOTS = 4
VMEM_LIMIT = 40 << 20


def swap(size, bit):
    return [(i, i ^ bit) for i in range(size)]


def unit_tile(units, shares):
    tile = units // sum(shares)
    return tile if tile * sum(shares) == units and tile % 128 == 0 else 0


def start(count, copies):
    for i in range(min(SLOTS, count)):
        for copy in copies(i, i):
            copy.start()


def stream(count, copies, work):
    def step(i, _):
        slot = lax.rem(i, SLOTS)
        for copy in copies(i, slot):
            copy.wait()
        work(i, slot)

        @pl.when(i + SLOTS < count)
        def _():
            for copy in copies(i + SLOTS, slot):
                copy.start()

        return 0

    lax.fori_loop(0, count, step, 0)


def up_kernel(first, count, tile, pieces, loads, *refs):
    parts, (gate, up), refs = refs[:pieces], refs[pieces : pieces + 2], refs[pieces + 2 :]
    outs, (x, held, sems, sem) = refs[:-4], refs[-4:]
    message, wide = outs[-2:] if pieces == 1 else outs[-3:-1]

    def copies(i, slot):
        columns = pl.ds(pl.multiple_of((first + i) * tile, tile), tile)
        return [
            pltpu.make_async_copy(w.at[:, columns], held.at[slot, j], sems.at[slot, j])
            for j, w in enumerate((gate, up))
        ]

    def place():
        rows = parts[0].shape[0]
        if pieces > 1:
            own = pltpu.make_async_copy(parts[0], x.at[:rows], sem)
            own.start()
            for j in range(1, pieces):
                x[j * rows : (j + 1) * rows] = parts[j][...]
            own.wait()
            outs[-1][...] = x[...]
        return x if pieces > 1 else parts[0]

    def work(i, slot):
        columns = pl.ds(pl.multiple_of(i * tile, tile), tile)
        for j in range(2):
            part = jnp.dot(rows[...], held[slot, j], preferred_element_type=F32)
            wide[j, :, columns] = part
            if not loads:
                message[j, :, columns] = part.astype(BF16)
            else:

                @pl.when(refs[0][0] == 0)
                def _():
                    message[j, :, columns] = part.astype(BF16)

    start(count, copies)
    rows = place()
    if loads:

        @pl.when(refs[0][0] > 0)
        def _():
            units, room = refs[1].shape[1], count * tile
            message[0, :, : min(units, room)] = refs[1][:, : min(units, room)]
            if units > room:
                message[1, :, : units - room] = refs[1][:, room:]

    stream(count, copies, work)


def partial_sums(parts, gate, up, first, count, tile, load, after):
    depth = gate.shape[0]
    rows = sum(part.shape[0] for part in parts)
    units = count * tile
    in_vmem, anywhere = pl.BlockSpec(memory_space=pltpu.VMEM), pl.BlockSpec(memory_space=pl.ANY)
    out_shape = [jax.ShapeDtypeStruct((2, rows, units), BF16), jax.ShapeDtypeStruct((2, rows, units), F32)]
    if len(parts) > 1:
        out_shape.append(jax.ShapeDtypeStruct((rows, depth), BF16))
    return pl.pallas_call(
        lambda *refs: up_kernel(first, count, tile, len(parts), bool(load), *refs),
        in_specs=[anywhere if len(parts) > 1 else in_vmem]
        + [in_vmem] * (len(parts) - 1)
        + [anywhere] * 2
        + ([pl.BlockSpec(memory_space=pltpu.SMEM), in_vmem] if load else [])
        + [anywhere] * len(after),
        out_specs=[in_vmem] * len(out_shape),
        out_shape=out_shape,
        scratch_shapes=[
            pltpu.VMEM((rows, depth) if len(parts) > 1 else (16, 128), BF16),
            pltpu.VMEM((SLOTS, 2, depth, tile), BF16),
            pltpu.SemaphoreType.DMA((SLOTS, 2)),
            pltpu.SemaphoreType.DMA,
        ],
        compiler_params=pltpu.CompilerParams(vmem_limit_bytes=VMEM_LIMIT),
        name="gate_up",
    )(*parts, gate, up, *load, *after)


def down_kernel(first, count, tile, inner, own, other, w, base, total, held, sems):
    room = other.shape[2] // tile

    def copies(i, slot):
        rows = pl.ds(pl.multiple_of((first + i) * tile, tile), tile)
        return [pltpu.make_async_copy(w.at[rows], held.at[slot], sems.at[slot])]

    def work(i, slot):
        columns = pl.ds(pl.multiple_of(i * tile, tile), tile)
        there = pl.ds(pl.multiple_of(lax.rem(i, room) * tile, tile), tile)
        h = jnp.where(inner[0] > 0, own[:, columns], other[lax.div(i, room), :, there])
        total[...] += jnp.dot(h, held[slot], preferred_element_type=F32)

    start(count, copies)
    total[...] = base[...]
    stream(count, copies, work)


def add_down(inner, own, other, down, base, first, count, tile):
    rows, width = base.shape
    in_vmem = pl.BlockSpec(memory_space=pltpu.VMEM)
    return pl.pallas_call(
        lambda *refs: down_kernel(first, count, tile, *refs),
        in_specs=[
            pl.BlockSpec(memory_space=pltpu.SMEM),
            in_vmem,
            in_vmem,
            pl.BlockSpec(memory_space=pl.ANY),
            in_vmem,
        ],
        out_specs=in_vmem,
        out_shape=jax.ShapeDtypeStruct((rows, width), F32),
        scratch_shapes=[pltpu.VMEM((SLOTS, tile, width), BF16), pltpu.SemaphoreType.DMA((SLOTS,))],
        compiler_params=pltpu.CompilerParams(vmem_limit_bytes=VMEM_LIMIT),
        name="down",
    )(inner, own, other, down, base)


def hold(value, *tokens):
    anywhere = pl.BlockSpec(memory_space=pl.ANY)
    return pl.pallas_call(
        lambda *refs: None,
        in_specs=[anywhere] * (1 + len(tokens)),
        out_specs=anywhere,
        out_shape=jax.ShapeDtypeStruct(value.shape, value.dtype),
        input_output_aliases={0: 0},
        compiler_params=pltpu.CompilerParams(vmem_limit_bytes=VMEM_LIMIT),
        name="hold",
    )(value, *tokens)


def keep_scale(keep_bits, width):
    shifts = jnp.arange(16, dtype=jnp.int32)
    keep = jnp.right_shift(keep_bits[:, :, None], shifts[None, None, :]) & 1
    return 2.0 * keep.reshape(keep_bits.shape[0], width).astype(F32)


def line_of_four(tensor):
    def shards(tokens, gate, up, down, keep_bits):
        rows = tokens.shape[0]
        units, width = down.shape
        tile = unit_tile(units, SHARES)
        inner = ((lax.axis_index("fsdp") + 1) // 2 == 1).astype(jnp.int32).reshape(1)
        scale = keep_scale(keep_bits, width)
        parts = [tokens]
        bits = [1 << b for b in reversed(range((tensor - 1).bit_length()))]
        for bit in bits:
            parts = parts + [lax.ppermute(part, "tensor", swap(tensor, bit)) for part in parts]
        count = len(SHARES)
        firsts = [sum(SHARES[:c]) for c in range(count)]
        wide, narrow, heard, side, crossed, kept, given = ([None] * count for _ in range(7))
        total = [jnp.zeros((rows * tensor, width), F32)]
        last = count - 1

        outward, across, back = [(0, 1), (3, 2)], [(1, 2), (2, 1)], [(1, 0), (2, 3)]

        def carries(c):
            return c >= LAG and SHARES[c - LAG] <= 2 * SHARES[c]

        def work_out(c):
            after = [side[c - 2]] if c >= 2 else []
            after += [kept[c - 3]] if c >= 3 else []
            after += [total[c - 4]] if c >= 5 else []
            load = [inner, kept[c - LAG]] if carries(c) else []
            out = partial_sums(parts, gate, up, firsts[c], SHARES[c], tile, load, after)
            wide[c] = out[1]
            parts[:] = out[2:] or parts
            heard[c] = lax.ppermute(out[0], "fsdp", outward + back if load else outward)
            if load:
                given[c - LAG] = heard[c]

        def add(c):
            wide[c] = wide[c] + heard[c].astype(F32)
            side[c] = wide[c].astype(BF16)
            crossed[c] = lax.ppermute(side[c], "fsdp", across)

        def finish(c):
            if c >= count - 3:
                wait = [side[count - 1]] if c == count - 3 else [kept[c - 1]]
                wait += [total[c - 2]]
                crossed[c] = hold(crossed[c], *wait)
            both = wide[c] + crossed[c].astype(F32)
            kept[c] = (jax.nn.silu(both[0]) * both[1]).astype(BF16)
            if c + LAG >= count or not carries(c + LAG):
                given[c] = lax.ppermute(kept[c], "fsdp", back)[None]

        def project(c):
            total.append(add_down(inner, kept[c], given[c], down, total[-1], firsts[c], SHARES[c], tile))

        for c in range(count + 1):
            if c < count:
                work_out(c)
            if c == count:
                heard[c - 1] = hold(heard[c - 1], side[c - 2])
            if c >= 1:
                add(c - 1)
            if 2 <= c and c - 2 < count - 3:
                finish(c - 2)
            if 4 <= c and c - 4 < count - 5:
                project(c - 4)
        for c in range(count - 3, count):
            while len(total) <= c - 2:
                project(len(total) - 1)
            finish(c)
        while len(total) <= count:
            project(len(total) - 1)
        total = total[-1]
        for step, bit in enumerate(reversed(bits)):
            half = total.shape[0] // 2
            away = total[half:]
            away = away if step == 0 else away.astype(BF16)
            total = total[:half] + lax.ppermute(away, "tensor", swap(tensor, bit)).astype(F32)
        return (scale * total).astype(BF16)

    return shards


def any_line(tokens, gate, up, down, keep_bits):
    units, width = down.shape
    x = lax.all_gather(tokens, "tensor", axis=0, tiled=True)
    both = jnp.concatenate(
        [jnp.dot(x, gate, preferred_element_type=F32), jnp.dot(x, up, preferred_element_type=F32)], axis=1
    )
    both = lax.psum_scatter(both, "fsdp", scatter_dimension=0, tiled=True)
    hidden = (jax.nn.silu(both[:, :units]) * both[:, units:]).astype(BF16)
    hidden = lax.all_gather(hidden, "fsdp", axis=0, tiled=True)
    total = jnp.dot(hidden, down, preferred_element_type=F32)
    total = lax.psum_scatter(total, "tensor", scatter_dimension=0, tiled=True)
    return (keep_scale(keep_bits, width) * total).astype(BF16)


def solution(mesh):
    tensor, fsdp = mesh.shape["tensor"], mesh.shape["fsdp"]

    def shards(tokens, gate, up, down, keep_bits):
        cut = fsdp == 4 and tensor & (tensor - 1) == 0 and unit_tile(down.shape[0], SHARES)
        return (line_of_four(tensor) if cut else any_line)(tokens, gate, up, down, keep_bits)

    return jax.shard_map(
        shards,
        mesh=mesh,
        in_specs=(
            P(("tensor", "dp"), "fsdp"),
            P("fsdp", "tensor"),
            P("fsdp", "tensor"),
            P("tensor", "fsdp"),
            P(("tensor", "dp"), "fsdp"),
        ),
        out_specs=P(("tensor", "dp"), "fsdp"),
        check_vma=False,
    )
```

```python
import jax
import jax.numpy as jnp
from jax import lax
from jax.experimental import pallas as pl
from jax.experimental.pallas import tpu as pltpu
from jax.sharding import PartitionSpec as P

F32, BF16 = jnp.float32, jnp.bfloat16
SHARES = (2, 5, 5, 5, 5, 4, 2)
LAG = 3
SLOTS = 6
VMEM_LIMIT = 40 << 20


def swap(size, bit):
    return [(i, i ^ bit) for i in range(size)]


def unit_tile(units, shares):
    tile = units // sum(shares)
    return tile if tile * sum(shares) == units and tile % 128 == 0 else 0


def start(count, copies):
    for i in range(min(SLOTS, count)):
        for copy in copies(i, i):
            copy.start()


def stream(count, copies, work):
    def step(i, _):
        slot = lax.rem(i, SLOTS)
        for copy in copies(i, slot):
            copy.wait()
        work(i, slot)

        @pl.when(i + SLOTS < count)
        def _():
            for copy in copies(i + SLOTS, slot):
                copy.start()

        return 0

    lax.fori_loop(0, count, step, 0)


def up_kernel(first, count, tile, pieces, loads, *refs):
    parts, (gate, up), refs = refs[:pieces], refs[pieces : pieces + 2], refs[pieces + 2 :]
    outs, (x, held, sems, sem) = refs[:-4], refs[-4:]
    message, wide = outs[-2:] if pieces == 1 else outs[-3:-1]

    def copies(i, slot):
        columns = pl.ds(pl.multiple_of((first + i) * tile, tile), tile)
        return [
            pltpu.make_async_copy(w.at[:, columns], held.at[slot, j], sems.at[slot, j])
            for j, w in enumerate((gate, up))
        ]

    def place():
        rows = parts[0].shape[0]
        if pieces > 1:
            own = pltpu.make_async_copy(parts[0], x.at[:rows], sem)
            own.start()
            for j in range(1, pieces):
                x[j * rows : (j + 1) * rows] = parts[j][...]
            own.wait()
            outs[-1][...] = x[...]
        return x if pieces > 1 else parts[0]

    def work(i, slot):
        columns = pl.ds(pl.multiple_of(i * tile, tile), tile)
        for j in range(2):
            part = jnp.dot(rows[...], held[slot, j], preferred_element_type=F32)
            wide[j, :, columns] = part
            if not loads:
                message[j, :, columns] = part.astype(BF16)
            else:

                @pl.when(refs[0][0] == 0)
                def _():
                    message[j, :, columns] = part.astype(BF16)

    start(count, copies)
    rows = place()
    if loads:

        @pl.when(refs[0][0] > 0)
        def _():
            units, room = refs[1].shape[1], count * tile
            message[0, :, : min(units, room)] = refs[1][:, : min(units, room)]
            if units > room:
                message[1, :, : units - room] = refs[1][:, room:]

    stream(count, copies, work)


def partial_sums(parts, gate, up, first, count, tile, load, after):
    depth = gate.shape[0]
    rows = sum(part.shape[0] for part in parts)
    units = count * tile
    in_vmem, anywhere = pl.BlockSpec(memory_space=pltpu.VMEM), pl.BlockSpec(memory_space=pl.ANY)
    out_shape = [jax.ShapeDtypeStruct((2, rows, units), BF16), jax.ShapeDtypeStruct((2, rows, units), F32)]
    if len(parts) > 1:
        out_shape.append(jax.ShapeDtypeStruct((rows, depth), BF16))
    return pl.pallas_call(
        lambda *refs: up_kernel(first, count, tile, len(parts), bool(load), *refs),
        in_specs=[anywhere if len(parts) > 1 else in_vmem]
        + [in_vmem] * (len(parts) - 1)
        + [anywhere] * 2
        + ([pl.BlockSpec(memory_space=pltpu.SMEM), in_vmem] if load else [])
        + [anywhere] * len(after),
        out_specs=[in_vmem] * len(out_shape),
        out_shape=out_shape,
        scratch_shapes=[
            pltpu.VMEM((rows, depth) if len(parts) > 1 else (16, 128), BF16),
            pltpu.VMEM((SLOTS, 2, depth, tile), BF16),
            pltpu.SemaphoreType.DMA((SLOTS, 2)),
            pltpu.SemaphoreType.DMA,
        ],
        compiler_params=pltpu.CompilerParams(vmem_limit_bytes=VMEM_LIMIT),
        name="gate_up",
    )(*parts, gate, up, *load, *after)


def down_kernel(first, count, tile, inner, own, other, w, base, total, held, sems):
    room = other.shape[2] // tile

    def copies(i, slot):
        rows = pl.ds(pl.multiple_of((first + i) * tile, tile), tile)
        return [pltpu.make_async_copy(w.at[rows], held.at[slot], sems.at[slot])]

    def work(i, slot):
        columns = pl.ds(pl.multiple_of(i * tile, tile), tile)
        there = pl.ds(pl.multiple_of(lax.rem(i, room) * tile, tile), tile)
        h = jnp.where(inner[0] > 0, own[:, columns], other[lax.div(i, room), :, there])
        total[...] += jnp.dot(h, held[slot], preferred_element_type=F32)

    start(count, copies)
    total[...] = base[...]
    stream(count, copies, work)


def add_down(inner, own, other, down, base, first, count, tile):
    rows, width = base.shape
    in_vmem = pl.BlockSpec(memory_space=pltpu.VMEM)
    return pl.pallas_call(
        lambda *refs: down_kernel(first, count, tile, *refs),
        in_specs=[
            pl.BlockSpec(memory_space=pltpu.SMEM),
            in_vmem,
            in_vmem,
            pl.BlockSpec(memory_space=pl.ANY),
            in_vmem,
        ],
        out_specs=in_vmem,
        out_shape=jax.ShapeDtypeStruct((rows, width), F32),
        scratch_shapes=[pltpu.VMEM((SLOTS, tile, width), BF16), pltpu.SemaphoreType.DMA((SLOTS,))],
        compiler_params=pltpu.CompilerParams(vmem_limit_bytes=VMEM_LIMIT),
        name="down",
    )(inner, own, other, down, base)


def hold(value, *tokens):
    anywhere = pl.BlockSpec(memory_space=pl.ANY)
    return pl.pallas_call(
        lambda *refs: None,
        in_specs=[anywhere] * (1 + len(tokens)),
        out_specs=anywhere,
        out_shape=jax.ShapeDtypeStruct(value.shape, value.dtype),
        input_output_aliases={0: 0},
        compiler_params=pltpu.CompilerParams(vmem_limit_bytes=VMEM_LIMIT),
        name="hold",
    )(value, *tokens)


def keep_scale(keep_bits, width):
    shifts = jnp.arange(16, dtype=jnp.int32)
    keep = jnp.right_shift(keep_bits[:, :, None], shifts[None, None, :]) & 1
    return 2.0 * keep.reshape(keep_bits.shape[0], width).astype(F32)


def line_of_four(tensor):
    def shards(tokens, gate, up, down, keep_bits):
        rows = tokens.shape[0]
        units, width = down.shape
        tile = unit_tile(units, SHARES)
        inner = ((lax.axis_index("fsdp") + 1) // 2 == 1).astype(jnp.int32).reshape(1)
        scale = keep_scale(keep_bits, width)
        parts = [tokens]
        bits = [1 << b for b in reversed(range((tensor - 1).bit_length()))]
        for bit in bits:
            parts = parts + [lax.ppermute(part, "tensor", swap(tensor, bit)) for part in parts]
        count = len(SHARES)
        firsts = [sum(SHARES[:c]) for c in range(count)]
        wide, narrow, heard, side, crossed, kept, given = ([None] * count for _ in range(7))
        total = [jnp.zeros((rows * tensor, width), F32)]
        last = count - 1

        outward, across, back = [(0, 1), (3, 2)], [(1, 2), (2, 1)], [(1, 0), (2, 3)]

        def carries(c):
            return c >= LAG and SHARES[c - LAG] <= 2 * SHARES[c]

        def work_out(c):
            after = [side[c - 2]] if c >= 2 else []
            after += [kept[c - 3]] if c >= 3 else []
            after += [total[c - 4]] if c >= 5 else []
            load = [inner, kept[c - LAG]] if carries(c) else []
            out = partial_sums(parts, gate, up, firsts[c], SHARES[c], tile, load, after)
            wide[c] = out[1]
            parts[:] = out[2:] or parts
            heard[c] = lax.ppermute(out[0], "fsdp", outward + back if load else outward)
            if load:
                given[c - LAG] = heard[c]

        def add(c):
            wide[c] = wide[c] + heard[c].astype(F32)
            side[c] = wide[c].astype(BF16)
            crossed[c] = lax.ppermute(side[c], "fsdp", across)

        def finish(c):
            if c == count - 3:
                crossed[c] = hold(crossed[c], side[count - 2])
            elif c > count - 3:
                crossed[c] = hold(crossed[c], side[count - 1], kept[c - 1], total[-1])
            both = wide[c] + crossed[c].astype(F32)
            kept[c] = (jax.nn.silu(both[0]) * both[1]).astype(BF16)
            if c + LAG >= count or not carries(c + LAG):
                given[c] = lax.ppermute(kept[c], "fsdp", back)[None]

        def project(c):
            total.append(add_down(inner, kept[c], given[c], down, total[-1], firsts[c], SHARES[c], tile))

        for c in range(count):
            work_out(c)
            if c >= 1:
                add(c - 1)
            if 2 <= c < count - 1:
                finish(c - 2)
            if 4 <= c < count - 1:
                project(c - 4)
        finish(count - 3)
        while len(total) <= count - 5:
            project(len(total) - 1)
        total[-1] = hold(total[-1], kept[count - 3])
        heard[count - 1] = hold(heard[count - 1], side[count - 2], kept[count - 3])
        add(count - 1)
        while len(total) <= count - 3:
            project(len(total) - 1)
        total[-1] = hold(total[-1], side[count - 1])
        finish(count - 2)
        finish(count - 1)
        while len(total) <= count:
            project(len(total) - 1)
        total = total[-1]
        for step, bit in enumerate(reversed(bits)):
            half = total.shape[0] // 2
            away = total[half:]
            away = away if step == 0 else away.astype(BF16)
            total = total[:half] + lax.ppermute(away, "tensor", swap(tensor, bit)).astype(F32)
        return (scale * total).astype(BF16)

    return shards


def any_line(tokens, gate, up, down, keep_bits):
    units, width = down.shape
    x = lax.all_gather(tokens, "tensor", axis=0, tiled=True)
    both = jnp.concatenate(
        [jnp.dot(x, gate, preferred_element_type=F32), jnp.dot(x, up, preferred_element_type=F32)], axis=1
    )
    both = lax.psum_scatter(both, "fsdp", scatter_dimension=0, tiled=True)
    hidden = (jax.nn.silu(both[:, :units]) * both[:, units:]).astype(BF16)
    hidden = lax.all_gather(hidden, "fsdp", axis=0, tiled=True)
    total = jnp.dot(hidden, down, preferred_element_type=F32)
    total = lax.psum_scatter(total, "tensor", scatter_dimension=0, tiled=True)
    return (keep_scale(keep_bits, width) * total).astype(BF16)


def solution(mesh):
    tensor, fsdp = mesh.shape["tensor"], mesh.shape["fsdp"]

    def shards(tokens, gate, up, down, keep_bits):
        cut = fsdp == 4 and tensor & (tensor - 1) == 0 and unit_tile(down.shape[0], SHARES)
        return (line_of_four(tensor) if cut else any_line)(tokens, gate, up, down, keep_bits)

    return jax.shard_map(
        shards,
        mesh=mesh,
        in_specs=(
            P(("tensor", "dp"), "fsdp"),
            P("fsdp", "tensor"),
            P("fsdp", "tensor"),
            P("tensor", "fsdp"),
            P(("tensor", "dp"), "fsdp"),
        ),
        out_specs=P(("tensor", "dp"), "fsdp"),
        check_vma=False,
    )
```

```python
import jax
import jax.numpy as jnp
from jax import lax
from jax.experimental import pallas as pl
from jax.experimental.pallas import tpu as pltpu
from jax.sharding import PartitionSpec as P

F32, BF16 = jnp.float32, jnp.bfloat16
SHARES = (2, 5, 5, 5, 5, 3, 3)
LAG = 3
SLOTS = 6
VMEM_LIMIT = 40 << 20


def swap(size, bit):
    return [(i, i ^ bit) for i in range(size)]


def unit_tile(units, shares):
    tile = units // sum(shares)
    return tile if tile * sum(shares) == units and tile % 128 == 0 else 0


def start(count, copies):
    for i in range(min(SLOTS, count)):
        for copy in copies(i, i):
            copy.start()


def stream(count, copies, work):
    def step(i, _):
        slot = lax.rem(i, SLOTS)
        for copy in copies(i, slot):
            copy.wait()
        work(i, slot)

        @pl.when(i + SLOTS < count)
        def _():
            for copy in copies(i + SLOTS, slot):
                copy.start()

        return 0

    lax.fori_loop(0, count, step, 0)


def up_kernel(first, count, tile, pieces, loads, *refs):
    parts, (gate, up), refs = refs[:pieces], refs[pieces : pieces + 2], refs[pieces + 2 :]
    outs, (x, held, sems, sem) = refs[:-4], refs[-4:]
    message, wide = outs[-2:] if pieces == 1 else outs[-3:-1]

    def copies(i, slot):
        columns = pl.ds(pl.multiple_of((first + i) * tile, tile), tile)
        return [
            pltpu.make_async_copy(w.at[:, columns], held.at[slot, j], sems.at[slot, j])
            for j, w in enumerate((gate, up))
        ]

    def place():
        rows = parts[0].shape[0]
        if pieces > 1:
            own = pltpu.make_async_copy(parts[0], x.at[:rows], sem)
            own.start()
            for j in range(1, pieces):
                x[j * rows : (j + 1) * rows] = parts[j][...]
            own.wait()
            outs[-1][...] = x[...]
        return x if pieces > 1 else parts[0]

    def work(i, slot):
        columns = pl.ds(pl.multiple_of(i * tile, tile), tile)
        for j in range(2):
            part = jnp.dot(rows[...], held[slot, j], preferred_element_type=F32)
            wide[j, :, columns] = part
            if not loads:
                message[j, :, columns] = part.astype(BF16)
            else:

                @pl.when(refs[0][0] == 0)
                def _():
                    message[j, :, columns] = part.astype(BF16)

    start(count, copies)
    rows = place()
    if loads:

        @pl.when(refs[0][0] > 0)
        def _():
            units, room = refs[1].shape[1], count * tile
            message[0, :, : min(units, room)] = refs[1][:, : min(units, room)]
            if units > room:
                message[1, :, : units - room] = refs[1][:, room:]

    stream(count, copies, work)


def partial_sums(parts, gate, up, first, count, tile, load, after):
    depth = gate.shape[0]
    rows = sum(part.shape[0] for part in parts)
    units = count * tile
    in_vmem, anywhere = pl.BlockSpec(memory_space=pltpu.VMEM), pl.BlockSpec(memory_space=pl.ANY)
    out_shape = [jax.ShapeDtypeStruct((2, rows, units), BF16), jax.ShapeDtypeStruct((2, rows, units), F32)]
    if len(parts) > 1:
        out_shape.append(jax.ShapeDtypeStruct((rows, depth), BF16))
    return pl.pallas_call(
        lambda *refs: up_kernel(first, count, tile, len(parts), bool(load), *refs),
        in_specs=[anywhere if len(parts) > 1 else in_vmem]
        + [in_vmem] * (len(parts) - 1)
        + [anywhere] * 2
        + ([pl.BlockSpec(memory_space=pltpu.SMEM), in_vmem] if load else [])
        + [anywhere] * len(after),
        out_specs=[in_vmem] * len(out_shape),
        out_shape=out_shape,
        scratch_shapes=[
            pltpu.VMEM((rows, depth) if len(parts) > 1 else (16, 128), BF16),
            pltpu.VMEM((SLOTS, 2, depth, tile), BF16),
            pltpu.SemaphoreType.DMA((SLOTS, 2)),
            pltpu.SemaphoreType.DMA,
        ],
        compiler_params=pltpu.CompilerParams(vmem_limit_bytes=VMEM_LIMIT),
        name="gate_up",
    )(*parts, gate, up, *load, *after)


def down_kernel(first, count, tile, inner, own, other, w, base, total, held, sems):
    room = other.shape[2] // tile

    def copies(i, slot):
        rows = pl.ds(pl.multiple_of((first + i) * tile, tile), tile)
        return [pltpu.make_async_copy(w.at[rows], held.at[slot], sems.at[slot])]

    def work(i, slot):
        columns = pl.ds(pl.multiple_of(i * tile, tile), tile)
        there = pl.ds(pl.multiple_of(lax.rem(i, room) * tile, tile), tile)
        h = jnp.where(inner[0] > 0, own[:, columns], other[lax.div(i, room), :, there])
        total[...] += jnp.dot(h, held[slot], preferred_element_type=F32)

    start(count, copies)
    total[...] = base[...]
    stream(count, copies, work)


def add_down(inner, own, other, down, base, first, count, tile):
    rows, width = base.shape
    in_vmem = pl.BlockSpec(memory_space=pltpu.VMEM)
    return pl.pallas_call(
        lambda *refs: down_kernel(first, count, tile, *refs),
        in_specs=[
            pl.BlockSpec(memory_space=pltpu.SMEM),
            in_vmem,
            in_vmem,
            pl.BlockSpec(memory_space=pl.ANY),
            in_vmem,
        ],
        out_specs=in_vmem,
        out_shape=jax.ShapeDtypeStruct((rows, width), F32),
        scratch_shapes=[pltpu.VMEM((SLOTS, tile, width), BF16), pltpu.SemaphoreType.DMA((SLOTS,))],
        compiler_params=pltpu.CompilerParams(vmem_limit_bytes=VMEM_LIMIT),
        name="down",
    )(inner, own, other, down, base)


def hold(value, *tokens):
    anywhere = pl.BlockSpec(memory_space=pl.ANY)
    return pl.pallas_call(
        lambda *refs: None,
        in_specs=[anywhere] * (1 + len(tokens)),
        out_specs=anywhere,
        out_shape=jax.ShapeDtypeStruct(value.shape, value.dtype),
        input_output_aliases={0: 0},
        compiler_params=pltpu.CompilerParams(vmem_limit_bytes=VMEM_LIMIT),
        name="hold",
    )(value, *tokens)


def keep_scale(keep_bits, width):
    shifts = jnp.arange(16, dtype=jnp.int32)
    keep = jnp.right_shift(keep_bits[:, :, None], shifts[None, None, :]) & 1
    return 2.0 * keep.reshape(keep_bits.shape[0], width).astype(F32)


def line_of_four(tensor):
    def shards(tokens, gate, up, down, keep_bits):
        rows = tokens.shape[0]
        units, width = down.shape
        tile = unit_tile(units, SHARES)
        inner = ((lax.axis_index("fsdp") + 1) // 2 == 1).astype(jnp.int32).reshape(1)
        scale = keep_scale(keep_bits, width)
        parts = [tokens]
        bits = [1 << b for b in reversed(range((tensor - 1).bit_length()))]
        for bit in bits:
            parts = parts + [lax.ppermute(part, "tensor", swap(tensor, bit)) for part in parts]
        count = len(SHARES)
        firsts = [sum(SHARES[:c]) for c in range(count)]
        wide, narrow, heard, side, crossed, kept, given = ([None] * count for _ in range(7))
        total = [jnp.zeros((rows * tensor, width), F32)]
        last = count - 1

        outward, across, back = [(0, 1), (3, 2)], [(1, 2), (2, 1)], [(1, 0), (2, 3)]

        def carries(c):
            return c >= LAG and SHARES[c - LAG] <= 2 * SHARES[c]

        def work_out(c):
            after = [side[c - 2]] if c >= 2 else []
            after += [kept[c - 3]] if c >= 3 else []
            after += [total[c - 4]] if c >= 5 else []
            load = [inner, kept[c - LAG]] if carries(c) else []
            out = partial_sums(parts, gate, up, firsts[c], SHARES[c], tile, load, after)
            wide[c] = out[1]
            parts[:] = out[2:] or parts
            heard[c] = lax.ppermute(out[0], "fsdp", outward + back if load else outward)
            if load:
                given[c - LAG] = heard[c]

        def add(c):
            wide[c] = wide[c] + heard[c].astype(F32)
            side[c] = wide[c].astype(BF16)
            crossed[c] = lax.ppermute(side[c], "fsdp", across)

        def finish(c):
            if c == count - 3:
                crossed[c] = hold(crossed[c], side[count - 2])
            elif c > count - 3:
                crossed[c] = hold(crossed[c], side[count - 1], kept[c - 1], total[-1])
            both = wide[c] + crossed[c].astype(F32)
            kept[c] = (jax.nn.silu(both[0]) * both[1]).astype(BF16)
            if c + LAG >= count or not carries(c + LAG):
                given[c] = lax.ppermute(kept[c], "fsdp", back)[None]

        def project(c):
            total.append(add_down(inner, kept[c], given[c], down, total[-1], firsts[c], SHARES[c], tile))

        for c in range(count):
            work_out(c)
            if c >= 1:
                add(c - 1)
            if 2 <= c < count - 1:
                finish(c - 2)
            if 4 <= c < count - 1:
                project(c - 4)
        finish(count - 3)
        while len(total) <= count - 5:
            project(len(total) - 1)
        total[-1] = hold(total[-1], kept[count - 3])
        heard[count - 1] = hold(heard[count - 1], side[count - 2], kept[count - 3])
        add(count - 1)
        while len(total) <= count - 3:
            project(len(total) - 1)
        total[-1] = hold(total[-1], side[count - 1])
        finish(count - 2)
        finish(count - 1)
        while len(total) <= count:
            project(len(total) - 1)
        total = total[-1]
        for step, bit in enumerate(reversed(bits)):
            half = total.shape[0] // 2
            away = total[half:]
            away = away if step == 0 else away.astype(BF16)
            total = total[:half] + lax.ppermute(away, "tensor", swap(tensor, bit)).astype(F32)
        return (scale * total).astype(BF16)

    return shards


def any_line(tokens, gate, up, down, keep_bits):
    units, width = down.shape
    x = lax.all_gather(tokens, "tensor", axis=0, tiled=True)
    both = jnp.concatenate(
        [jnp.dot(x, gate, preferred_element_type=F32), jnp.dot(x, up, preferred_element_type=F32)], axis=1
    )
    both = lax.psum_scatter(both, "fsdp", scatter_dimension=0, tiled=True)
    hidden = (jax.nn.silu(both[:, :units]) * both[:, units:]).astype(BF16)
    hidden = lax.all_gather(hidden, "fsdp", axis=0, tiled=True)
    total = jnp.dot(hidden, down, preferred_element_type=F32)
    total = lax.psum_scatter(total, "tensor", scatter_dimension=0, tiled=True)
    return (keep_scale(keep_bits, width) * total).astype(BF16)


def solution(mesh):
    tensor, fsdp = mesh.shape["tensor"], mesh.shape["fsdp"]

    def shards(tokens, gate, up, down, keep_bits):
        cut = fsdp == 4 and tensor & (tensor - 1) == 0 and unit_tile(down.shape[0], SHARES)
        return (line_of_four(tensor) if cut else any_line)(tokens, gate, up, down, keep_bits)

    return jax.shard_map(
        shards,
        mesh=mesh,
        in_specs=(
            P(("tensor", "dp"), "fsdp"),
            P("fsdp", "tensor"),
            P("fsdp", "tensor"),
            P("tensor", "fsdp"),
            P(("tensor", "dp"), "fsdp"),
        ),
        out_specs=P(("tensor", "dp"), "fsdp"),
        check_vma=False,
    )
```
